1024 devices in a mesh: row: 16 (over z), col: 64 (over y, x, core).
Axes of the slice: x: 4, y: 8, z: 16, core: 2. Of those that a mesh axis runs over, the one named last changes fastest.
Arguments:
- densities: bfloat16 [16384, 32, 256], P(('row', 'col')), may hold values from -6 to 6
- points: bfloat16 [16384, 3, 256], P(('row', 'col')), may hold values from 0 to 1
- normals: bfloat16 [16384, 3, 256], P(('row', 'col')), may hold values from -1.1953125 to 1.1953125
- source_basis: bfloat16 [16384, 64, 256], P(('row', 'col')), may hold values from -0.375 to 0.375
- target_basis: bfloat16 [16384, 64, 256], P(('row', 'col')), may hold values from -0.75 to 0.75
- upward: bfloat16 [16384, 64, 64], P(('row', 'col')), may hold values from -0.1875 to 0.1875
- downward: bfloat16 [16384, 64, 64], P(('row', 'col')), may hold values from -0.75 to 0.75
- couplings: bfloat16 [16384, 8, 64, 64], P(('row', 'col')), may hold values from -0.25 to 0.25
- coarse_couplings: bfloat16 [16, 64, 4, 64, 64], P('row', 'col'), may hold values from -0.1875 to 0.1875
- near_list: int32 [16384, 12], P(('row', 'col')), may hold values from 0 to 47, as said below
- far_want: int32 [16, 64, 64, 2], P('row', 'col'), may hold values from 0 to 15, as said below
- far_list: int32 [16384, 8], P(('row', 'col')), may hold values from 0 to 127, as said below
- far_count: int32 [16384], P(('row', 'col')), may hold values from 4 to 8
Outputs:
- potentials: float32 [16384, 32, 256], P(('row', 'col'))
The draws below stay inside these ranges and needn't reach their ends.
Inputs may be any that keep to these rules, and one draw needn't show every extreme that they name: `near_list`: entry 0 of leaf i is 16 + i mod 16; the entries of one leaf are distinct. `far_want`: the 2 entries of one [g, c, p] are distinct. `far_list`: on each device every value appears exactly 16 * 8 / 128 times.
All inputs are finite; a program needn't handle non-finite values.
Results may differ from the reference program's by a relative error of at most 0.0029.
Values may be sent and summed in bfloat16 or wider, within the bound.
A program may use at most 32 MiB of HBM per device.

```python
import math
import jax
import jax.numpy as jnp
from jax import lax

LEAF = 256
RANK = 64
RHS = 32
L_DEV = 16
NEAR = 12
FAR = 8
FCAP = 2
GROUPS = 16
PEERS = 64
LEAVES = 16384
LEVELS = 4


def draw_near_list(key, part):
    key = jax.random.fold_in(key, 11)
    pool_size = 3 * L_DEV
    leaf_keys = jax.random.split(key, LEAVES)

    def one_leaf(leaf_key, owner):
        shuffled = jax.random.permutation(leaf_key, pool_size - 1).astype(jnp.int32)
        picked = shuffled[:NEAR - 1]
        picked = jnp.where(picked >= owner, picked + 1, picked)
        return jnp.concatenate([owner[None], picked]).astype(jnp.int32)
    owners = (L_DEV + jnp.arange(LEAVES, dtype=jnp.int32) % L_DEV).astype(jnp.int32)
    return jax.vmap(one_leaf)(leaf_keys, owners)


def draw_far_want(key, part):
    key = jax.random.fold_in(key, 23)
    pair_keys = jax.random.split(key, GROUPS * PEERS * PEERS)

    def one_pair(pair_key):
        return jax.random.permutation(pair_key, L_DEV)[:FCAP].astype(jnp.int32)
    chosen = jax.vmap(one_pair)(pair_keys)
    return chosen.reshape(GROUPS, PEERS, PEERS, FCAP).astype(jnp.int32)


def draw_far_list(key, part):
    key = jax.random.fold_in(key, 37)
    device_keys = jax.random.split(key, GROUPS * PEERS)

    def one_device(device_key):
        shuffled = jax.random.permutation(device_key, L_DEV * FAR).astype(jnp.int32)
        return (shuffled % (PEERS * FCAP)).reshape(L_DEV, FAR)
    return jax.vmap(one_device)(device_keys).reshape(LEAVES, FAR).astype(jnp.int32)


def place_ends(values, rng, smallest, high):
    dims = values.shape
    place = [jax.random.randint(jax.random.fold_in(rng, axis), (), 0, dims[axis]) for axis in range(len(dims))]
    values = values.at[tuple(place)].set(smallest)
    longest = dims.index(max(dims))
    place[longest] = (place[longest] + 1) % dims[longest]
    return values.at[tuple(place)].set(high)


def level_of(rng, shape, cuts, least, top_value):
    loudness = 1.0
    for position, parts in cuts:
        draws = jax.random.uniform(jax.random.fold_in(jax.random.fold_in(rng, 6), position), (parts,), jnp.float32, least / len(cuts), top_value / len(cuts))
        loudness = loudness * jnp.repeat(jnp.exp(draws), shape[position] // parts).reshape((-1,) + (1,) * (len(shape) - 1 - position))
    return loudness


def gaussian(stream_key, extent, width, most, pieces=(), kind=jnp.bfloat16):
    array = width * jax.random.normal(stream_key, extent, jnp.float32)
    if pieces:
        array = array * level_of(stream_key, extent, pieces, -0.22, 0.18)
    return jnp.clip(array, -most, most).astype(kind)


def setup_inputs(seed: int = 0) -> dict:
    key_list = jax.random.split(jax.random.key(seed), 14)
    return {
        "densities": gaussian(key_list[0], (LEAVES, RHS, LEAF), 1.0, 6.0, ((0, 1024),)),
        "points": jnp.clip(1.0 * jax.random.uniform(key_list[1], (LEAVES, 3, LEAF), jnp.float32) ** level_of(key_list[1], (LEAVES, 3, LEAF), ((0, 1024),), -0.2, 0.2), 0.0, 1.0).astype(jnp.bfloat16),
        "normals": gaussian(key_list[2], (LEAVES, 3, LEAF), 0.2, 1.1953125, ((0, 1024),)),
        "source_basis": gaussian(key_list[3], (LEAVES, RANK, LEAF), LEAF ** -0.5, 0.375, ((0, 1024),)),
        "target_basis": gaussian(key_list[4], (LEAVES, RANK, LEAF), RANK ** -0.5, 0.75, ((0, 1024),)),
        "upward": gaussian(key_list[5], (LEAVES, RANK, RANK), (RANK * L_DEV) ** -0.5, 0.1875, ((0, 1024),)),
        "downward": gaussian(key_list[6], (LEAVES, RANK, RANK), RANK ** -0.5, 0.75, ((0, 1024),)),
        "couplings": gaussian(key_list[7], (LEAVES, FAR, RANK, RANK), (RANK * FAR) ** -0.5, 0.25, ((0, 1024),)),
        "coarse_couplings": gaussian(key_list[8], (GROUPS, PEERS, LEVELS, RANK, RANK), (RANK * GROUPS) ** -0.5, 0.1875, ((0, 16), (1, 64))),
        "near_list": draw_near_list(jax.random.fold_in(key_list[13], 71), 0),
        "far_want": draw_far_want(jax.random.fold_in(key_list[13], 71), 0),
        "far_list": draw_far_list(jax.random.fold_in(key_list[13], 71), 0),
        "far_count": place_ends(jax.random.randint(key_list[12], (LEAVES,), FAR // 2, FAR + 1), jax.random.fold_in(key_list[12], 1), FAR // 2, FAR).astype(jnp.int32),
    }


soften_square = 0.0025
kernel_scale = 0.25 / math.pi

def near_tile(target_points, source_points, source_normals):
    target = target_points.astype(jnp.float32)
    source = source_points.astype(jnp.float32)
    normal = source_normals.astype(jnp.float32)
    delta_x = target[0][None, None, :] - source[:, 0, :, None]
    delta_y = target[1][None, None, :] - source[:, 1, :, None]
    delta_z = target[2][None, None, :] - source[:, 2, :, None]
    squared = delta_x * delta_x + delta_y * delta_y + delta_z * delta_z + soften_square
    normal_dot = normal[:, 0, :, None] * delta_x + normal[:, 1, :, None] * delta_y + normal[:, 2, :, None] * delta_z
    return (kernel_scale * normal_dot * lax.rsqrt(squared) / squared).astype(jnp.bfloat16)

def reference(densities, points, normals, source_basis, target_basis, upward, downward, couplings, coarse_couplings, near_list, far_want, far_list, far_count):
    leaf_ids = jnp.arange(LEAVES, dtype=jnp.int32)
    device_ids = leaf_ids // L_DEV
    group_ids = device_ids // PEERS
    column_ids = device_ids % PEERS
    near_column = (column_ids[:, None] + near_list // L_DEV - 1 + PEERS) % PEERS
    near_source = ((group_ids[:, None] * PEERS + near_column) * L_DEV + near_list % L_DEV).astype(jnp.int32)

    def near_leaf(inputs):
        target_points, source_ids = inputs
        kernel_tile = near_tile(target_points, points[source_ids], normals[source_ids])
        return jnp.einsum('krq,kqp->rp', densities[source_ids].astype(jnp.float32), kernel_tile.astype(jnp.float32))
    near_part = lax.map(near_leaf, (points, near_source))

    def skeleton_leaf(inputs):
        values, basis = inputs
        return jnp.dot(values, basis.T, preferred_element_type=jnp.float32).astype(jnp.bfloat16)
    skeleton = lax.map(skeleton_leaf, (densities, source_basis))
    peer_ids = far_list // FCAP
    slot_ids = far_list % FCAP
    local_ids = far_want[group_ids[:, None], column_ids[:, None], peer_ids, slot_ids]
    far_source = ((group_ids[:, None] * PEERS + peer_ids) * L_DEV + local_ids).astype(jnp.int32)
    far_coeff = jnp.zeros((LEAVES, RHS, RANK), jnp.float32)
    for entry in range(FAR):
        chosen = skeleton[far_source[:, entry]].astype(jnp.float32)
        product = jnp.einsum('lrm,lmn->lrn', chosen, couplings[:, entry].astype(jnp.float32))
        active = (entry < far_count)[:, None, None]
        far_coeff = far_coeff + jnp.where(active, product, jnp.zeros_like(product))
    upward_terms = jnp.einsum('lrm,lmn->lrn', skeleton.astype(jnp.float32), upward.astype(jnp.float32))
    device_sums = upward_terms.reshape(GROUPS, PEERS, L_DEV, RHS, RANK).sum(axis=2)
    row_ids = jnp.arange(GROUPS, dtype=jnp.int32)
    coarse_sum = jnp.zeros((GROUPS, PEERS, RHS, RANK), jnp.float32)
    for level in range(LEVELS):
        in_sibling = (row_ids[None, :] >> level == row_ids[:, None] >> level ^ 1).astype(jnp.float32)
        sibling_sum = jnp.einsum('gh,hcrm->gcrm', in_sibling, device_sums, precision=lax.Precision.HIGHEST)
        coarse_sum = coarse_sum + jnp.einsum('gcrm,gcmn->gcrn', sibling_sum, coarse_couplings[:, :, level].astype(jnp.float32), precision=lax.Precision.HIGHEST)
    coarse_field = coarse_sum.astype(jnp.bfloat16)
    leaf_field = coarse_field.reshape(GROUPS * PEERS, RHS, RANK)[device_ids].astype(jnp.float32)
    leaf_coeff = (far_coeff + jnp.einsum('lrm,lmn->lrn', leaf_field, downward.astype(jnp.float32))).astype(jnp.bfloat16)
    far_part = jnp.einsum('lrm,lmq->lrq', leaf_coeff.astype(jnp.float32), target_basis.astype(jnp.float32))
    return near_part + far_part
```

```python
import math

import jax
import jax.numpy as jnp
from jax import lax
from jax.experimental import pallas as pl
from jax.experimental.pallas import tpu as pltpu
from jax.sharding import PartitionSpec as P

soften_square = 0.0025
kernel_scale = 0.25 / math.pi

LEAVES = 16
RHS = 32
RANK = 64
LEAF = 256
NEAR = 12
FAR = 8
SLOTS = 2
LEVELS = 4
ROWS = 16
COLS = 64
DEPTH = 16
VECTOR_ROWS = 192

f32 = jnp.float32
bf16 = jnp.bfloat16
MESH = pl.DeviceIdType.MESH
CONTRACT_LAST = (((1,), (1,)), ((), ()))


def split3(value):
    high = value.astype(bf16).astype(f32)
    rest = value - high
    middle = rest.astype(bf16).astype(f32)
    return high, middle, rest - middle


def kernel(
    densities, points, normals, source_basis, target_basis, upward, downward, couplings,
    coarse_couplings, near_list, far_want, far_list, far_count,
    out,
    dens, geom, wants_own, wants, asked, sbasis, tbasis, up, down, coup, coarse_coup,
    nlist, flist, fcount, skel, outgoing, received, sums, features, sources, rows, columns, result,
    load_sem, small_sem, halo_send, halo_recv, want_send, want_recv, far_send, far_recv,
    sum_send, sum_recv, out_sem,
):
    g = lax.axis_index("row")
    c = lax.axis_index("col")
    above = lax.rem(c + 1, COLS)
    below = lax.rem(c + COLS - 1, COLS)

    def load(source, target, sem):
        copy = pltpu.make_async_copy(source, target, sem)
        copy.start()
        return copy

    load_points = load(points, geom.at[1, pl.ds(0, 3)], load_sem.at[0])
    load_normals = load(normals, geom.at[1, pl.ds(3, 3)], load_sem.at[1])
    load_dens = load(densities, dens.at[1], load_sem.at[2])
    load_wants = load(far_want, wants_own, load_sem.at[3])
    load_sbasis = load(source_basis, sbasis, load_sem.at[4])
    load_up = load(upward, up, load_sem.at[5])
    load_nlist = load(near_list, nlist, small_sem.at[0])
    load_flist = load(far_list, flist, small_sem.at[1])
    load_fcount = load(far_count, fcount, small_sem.at[2])
    load_coarse = load(coarse_couplings, coarse_coup, load_sem.at[6])
    load_coup = load(couplings, coup, load_sem.at[7])
    load_down = load(downward, down, load_sem.at[8])
    load_tbasis = load(target_basis, tbasis, load_sem.at[9])

    barrier = pltpu.get_barrier_semaphore()

    def greet_col(d, _):
        pl.semaphore_signal(
            barrier, inc=1, device_id=(g, lax.rem(c + d, COLS)), device_id_type=MESH
        )
        return 0

    def greet_row(d, _):
        pl.semaphore_signal(
            barrier, inc=1, device_id=(lax.rem(g + d, ROWS), c), device_id_type=MESH
        )
        return 0

    lax.fori_loop(1, COLS, greet_col, 0)
    lax.fori_loop(1, ROWS, greet_row, 0)

    load_points.wait()
    load_normals.wait()
    load_dens.wait()
    load_wants.wait()
    pl.semaphore_wait(barrier, COLS + ROWS - 2)

    halo = []
    for index, (buffer, slot, target) in enumerate(
        ((geom, 0, above), (geom, 2, below), (dens, 0, above), (dens, 2, below))
    ):
        copy = pltpu.make_async_remote_copy(
            src_ref=buffer.at[1],
            dst_ref=buffer.at[slot],
            send_sem=halo_send.at[index],
            recv_sem=halo_recv.at[index],
            device_id=(g, target),
            device_id_type=MESH,
        )
        copy.start()
        halo.append(copy)

    def send_want(d, _):
        pltpu.make_async_remote_copy(
            src_ref=wants_own,
            dst_ref=wants.at[c],
            send_sem=want_send,
            recv_sem=want_recv,
            device_id=(g, lax.rem(c + d, COLS)),
            device_id_type=MESH,
        ).start()
        return 0

    lax.fori_loop(1, COLS, send_want, 0)

    load_sbasis.wait()
    load_up.wait()

    total = jnp.zeros((RHS, RANK), f32)
    for leaf in range(LEAVES):
        value = lax.dot_general(
            dens[1, leaf], sbasis[leaf], CONTRACT_LAST, preferred_element_type=f32
        )
        rounded = value.astype(bf16)
        value = rounded.astype(f32)
        skel[leaf] = jnp.concatenate([value[:16], value[16:]], axis=1).astype(bf16)
        total = total + jnp.dot(rounded, up[leaf], preferred_element_type=f32)
    sums[g] = jnp.concatenate([total[:16], total[16:]], axis=1)

    def send_sum(d, _):
        pltpu.make_async_remote_copy(
            src_ref=sums.at[g],
            dst_ref=sums.at[g],
            send_sem=sum_send,
            recv_sem=sum_recv,
            device_id=(lax.rem(g + d, ROWS), c),
            device_id_type=MESH,
        ).start()
        return 0

    lax.fori_loop(1, ROWS, send_sum, 0)

    zero = jnp.zeros((LEAVES, LEAF), f32)
    one = jnp.ones((LEAVES, LEAF), f32)

    def put(row, first, second):
        for part, value in enumerate((first, second)):
            for half in range(2):
                features[2 * part + half, pl.ds(row * LEAVES, LEAVES)] = value[
                    :, half * 128 : half * 128 + 128
                ]

    def gathered(leaf, parts):
        return jnp.concatenate(
            [features[part, pl.ds(leaf, DEPTH, stride=LEAVES), :] for part in parts], axis=1
        )

    def source_features(block):
        x, y, z = (geom[block, d].astype(f32) for d in range(3))
        nx, ny, nz = (kernel_scale * geom[block, 3 + d].astype(f32) for d in range(3))
        square = x * x + y * y + z * z + soften_square
        along = nx * x + ny * y + nz * z
        for d, value in enumerate((nx, ny, nz, along)):
            rows[d, pl.ds(block * LEAVES, LEAVES)] = value
        sh, sm, sl = split3(square)
        ah, am, al = split3(-along)
        xh, xm, xl = split3(nx)
        yh, ym, yl = split3(ny)
        zh, zm, zl = split3(nz)
        for row, (first, second) in enumerate((
            (-2.0 * x, xh), (-2.0 * y, yh), (-2.0 * z, zh), (sh, ah), (sm, am), (sl, al),
            (one, zero), (one, zero), (one, zero), (zero, xm), (zero, ym), (zero, zm),
            (zero, xl), (zero, yl), (zero, zl), (zero, zero),
        )):
            put(row, first, second)

        def one_leaf(leaf, _):
            sources[block * LEAVES + leaf] = gathered(leaf, range(4)).astype(bf16)
            return 0

        lax.fori_loop(0, LEAVES, one_leaf, 0, unroll=4)

    source_features(1)

    wants[c] = wants_own[...]
    pltpu.make_async_remote_copy(
        src_ref=wants.at[pl.ds(0, COLS - 1)],
        dst_ref=wants.at[pl.ds(0, COLS - 1)],
        send_sem=want_send,
        recv_sem=want_recv,
        device_id=(g, above),
        device_id_type=MESH,
    ).wait_recv()

    read_wants = load(wants, asked, small_sem.at[3])
    read_wants.wait()

    def answer(d, _):
        peer = lax.rem(c + d, COLS)
        for slot in range(SLOTS):
            outgoing[SLOTS * peer + slot] = skel[asked[peer, slot, c]]
        pltpu.make_async_remote_copy(
            src_ref=outgoing.at[pl.ds(SLOTS * peer, SLOTS)],
            dst_ref=received.at[pl.ds(SLOTS * c, SLOTS)],
            send_sem=far_send,
            recv_sem=far_recv,
            device_id=(g, peer),
            device_id_type=MESH,
        ).start()
        return 0

    lax.fori_loop(1, COLS, answer, 0)
    for slot in range(SLOTS):
        received[SLOTS * c + slot] = skel[asked[c, slot, c]]

    for copy in halo:
        copy.wait_recv()
    source_features(0)
    source_features(2)

    load_nlist.wait()
    px, py, pz = (geom[1, d].astype(f32) for d in range(3))
    th, tm, tl = split3(px * px + py * py + pz * pz)
    for row, value in enumerate(
        (px, py, pz, one, one, one, th, tm, tl, px, py, pz, px, py, pz, zero)
    ):
        put(row, value, zero)

    def near_leaf(leaf, _):
        target = gathered(leaf, range(2)).T
        for d in range(3):
            columns[d] = jnp.broadcast_to(target[:VECTOR_ROWS, d : d + 1], (VECTOR_ROWS, 128))
        target = target.astype(bf16)

        def geometry(q):
            source = sources[q]
            square = jnp.dot(target, source[:, :LEAF], preferred_element_type=f32)
            row = [rows[d, pl.ds(q, 1), :] for d in range(4)]
            parts = []
            for start in range(0, LEAF, 128):
                nx, ny, nz, along = (value[:, start : start + 128] for value in row)
                parts.append(columns[0] * nx + columns[1] * ny + columns[2] * nz - along)
            normal = jnp.concatenate(parts, axis=1)
            rest = jnp.dot(target[VECTOR_ROWS:], source[:, LEAF:], preferred_element_type=f32)
            return square, jnp.concatenate([normal, rest], axis=0)

        total = jnp.zeros((RHS, LEAF), f32)
        held = geometry(nlist[leaf, 0])
        for entry in range(NEAR):
            q = nlist[leaf, entry]
            square, normal = held
            if entry < NEAR - 1:
                held = geometry(nlist[leaf, entry + 1])
            inverse = lax.rsqrt(square)
            tile = ((normal * inverse) * (inverse * inverse)).astype(bf16)
            total = total + lax.dot_general(
                dens[q // LEAVES, q % LEAVES], tile, CONTRACT_LAST, preferred_element_type=f32
            )
        result[leaf] = total
        return 0

    lax.fori_loop(0, LEAVES, near_leaf, 0)

    load_coarse.wait()
    pltpu.make_async_remote_copy(
        src_ref=sums.at[pl.ds(0, ROWS - 1)],
        dst_ref=sums.at[pl.ds(0, ROWS - 1)],
        send_sem=sum_send,
        recv_sem=sum_recv,
        device_id=(lax.rem(g + 1, ROWS), c),
        device_id_type=MESH,
    ).wait_recv()
    siblings = []
    for level in range(LEVELS):
        width = 2**level
        block = g // width
        first = (block + 1 - 2 * lax.rem(block, 2)) * width
        value = sums[first]
        for other in range(1, width):
            value = value + sums[first + other]
        siblings.append(value)
    mixed = jnp.concatenate(
        [
            jnp.concatenate([value[:, :RANK] for value in siblings], axis=1),
            jnp.concatenate([value[:, RANK:] for value in siblings], axis=1),
        ],
        axis=0,
    )
    pieces = jnp.concatenate(split3(mixed), axis=0).astype(bf16)
    products = jnp.dot(
        pieces, coarse_coup[...].reshape(LEVELS * RANK, RANK), preferred_element_type=f32
    )
    field = ((products[2 * RHS :] + products[RHS : 2 * RHS]) + products[:RHS]).astype(bf16)

    load_flist.wait()
    load_fcount.wait()
    load_coup.wait()
    load_down.wait()
    load_tbasis.wait()
    pltpu.make_async_remote_copy(
        src_ref=received.at[pl.ds(0, SLOTS * (COLS - 1))],
        dst_ref=received.at[pl.ds(0, SLOTS * (COLS - 1))],
        send_sem=far_send,
        recv_sem=far_recv,
        device_id=(g, above),
        device_id_type=MESH,
    ).wait_recv()

    def far_leaf(leaf, _):
        count = fcount[leaf]
        upper, lower = [], []
        for entry in range(FAR):
            value = received[flist[entry, leaf]].astype(f32)
            value = jnp.where(entry < count, value, jnp.zeros_like(value))
            upper.append(value[:, :RANK])
            lower.append(value[:, RANK:])
        chosen = jnp.concatenate(
            [jnp.concatenate(upper, axis=1), jnp.concatenate(lower, axis=1)], axis=0
        ).astype(bf16)
        coeff = jnp.dot(
            chosen, coup[leaf].reshape(FAR * RANK, RANK), preferred_element_type=f32
        ) + jnp.dot(field, down[leaf], preferred_element_type=f32)
        result[leaf] = result[leaf] + jnp.dot(
            coeff.astype(bf16), tbasis[leaf], preferred_element_type=f32
        )
        return 0

    lax.fori_loop(0, LEAVES, far_leaf, 0, unroll=4)
    store = pltpu.make_async_copy(result, out, out_sem)
    store.start()

    for copy in halo:
        copy.wait_send()
    pltpu.make_async_remote_copy(
        src_ref=received.at[pl.ds(0, SLOTS * (COLS - 1))],
        dst_ref=received.at[pl.ds(0, SLOTS * (COLS - 1))],
        send_sem=far_send,
        recv_sem=far_recv,
        device_id=(g, above),
        device_id_type=MESH,
    ).wait_send()
    pltpu.make_async_remote_copy(
        src_ref=sums.at[pl.ds(0, ROWS - 1)],
        dst_ref=sums.at[pl.ds(0, ROWS - 1)],
        send_sem=sum_send,
        recv_sem=sum_recv,
        device_id=(lax.rem(g + 1, ROWS), c),
        device_id_type=MESH,
    ).wait_send()

    def sent_want(d, _):
        pltpu.make_async_remote_copy(
            src_ref=wants_own,
            dst_ref=wants.at[c],
            send_sem=want_send,
            recv_sem=want_recv,
            device_id=(g, above),
            device_id_type=MESH,
        ).wait_send()
        return 0

    lax.fori_loop(1, COLS, sent_want, 0)
    store.wait()


def local(
    densities, points, normals, source_basis, target_basis, upward, downward, couplings,
    coarse_couplings, near_list, far_want, far_list, far_count,
):
    anywhere = pl.BlockSpec(memory_space=pl.ANY)
    dma = pltpu.SemaphoreType.DMA
    return pl.pallas_call(
        kernel,
        out_shape=jax.ShapeDtypeStruct((LEAVES, RHS, LEAF), f32),
        in_specs=[anywhere] * 13,
        out_specs=anywhere,
        scratch_shapes=[
            pltpu.VMEM((3, LEAVES, RHS, LEAF), bf16),
            pltpu.VMEM((3, 6, LEAVES, LEAF), bf16),
            pltpu.VMEM((SLOTS, COLS), jnp.int32),
            pltpu.VMEM((COLS, SLOTS, COLS), jnp.int32),
            pltpu.SMEM((COLS, SLOTS, COLS), jnp.int32),
            pltpu.VMEM((LEAVES, RANK, LEAF), bf16),
            pltpu.VMEM((LEAVES, RANK, LEAF), bf16),
            pltpu.VMEM((LEAVES, RANK, RANK), bf16),
            pltpu.VMEM((LEAVES, RANK, RANK), bf16),
            pltpu.VMEM((LEAVES, FAR, RANK, RANK), bf16),
            pltpu.VMEM((LEVELS, RANK, RANK), bf16),
            pltpu.SMEM((LEAVES, NEAR), jnp.int32),
            pltpu.SMEM((FAR, LEAVES), jnp.int32),
            pltpu.SMEM((LEAVES,), jnp.int32),
            pltpu.VMEM((LEAVES, 16, 128), bf16),
            pltpu.VMEM((SLOTS * COLS, 16, 128), bf16),
            pltpu.VMEM((SLOTS * COLS, 16, 128), bf16),
            pltpu.VMEM((ROWS, 16, 128), f32),
            pltpu.VMEM((4, DEPTH * LEAVES, 128), f32),
            pltpu.VMEM((3 * LEAVES, DEPTH, 2 * LEAF), bf16),
            pltpu.VMEM((4, 3 * LEAVES, LEAF), f32),
            pltpu.VMEM((3, VECTOR_ROWS, 128), f32),
            pltpu.VMEM((LEAVES, RHS, LEAF), f32),
            dma((10,)), dma((4,)), dma((4,)), dma((4,)), dma, dma, dma, dma, dma, dma, dma,
        ],
        compiler_params=pltpu.CompilerParams(
            collective_id=0, has_side_effects=True, vmem_limit_bytes=60 * 2**20
        ),
        cost_estimate=pl.CostEstimate(
            flops=2 * 16 * 12 * 65536 * 48, bytes_accessed=6 * 2**20, transcendentals=16 * 12 * 65536
        ),
        name="h2_product",
    )(
        densities,
        points.transpose(1, 0, 2),
        normals.transpose(1, 0, 2),
        source_basis,
        target_basis,
        upward,
        downward,
        couplings,
        coarse_couplings.reshape(LEVELS, RANK, RANK),
        near_list,
        far_want.reshape(COLS, SLOTS).T,
        far_list.T,
        far_count,
    )


def solution(mesh):
    leaf = P(("row", "col"), None, None)
    placed = (
        (leaf,) * 7
        + (P(("row", "col"), None, None, None), P("row", "col", None, None, None))
        + (P(("row", "col"), None), P("row", "col", None, None))
        + (P(("row", "col"), None), P(("row", "col")))
    )
    return jax.shard_map(local, mesh=mesh, in_specs=placed, out_specs=leaf, check_vma=False)
```

```python
import math

import jax
import jax.numpy as jnp
from jax import lax
from jax.experimental import pallas as pl
from jax.experimental.pallas import tpu as pltpu
from jax.sharding import PartitionSpec as P

soften_square = 0.0025
kernel_scale = 0.25 / math.pi

LEAVES = 16
RHS = 32
RANK = 64
LEAF = 256
NEAR = 12
FAR = 8
SLOTS = 2
LEVELS = 4
ROWS = 16
COLS = 64
DEPTH = 16
SELF_GROUP = 8
NEAR_GROUP = 4
VECTOR_ROWS = 128

f32 = jnp.float32
bf16 = jnp.bfloat16
MESH = pl.DeviceIdType.MESH
CONTRACT_LAST = (((1,), (1,)), ((), ()))


def split3(value):
    high = value.astype(bf16).astype(f32)
    rest = value - high
    middle = rest.astype(bf16).astype(f32)
    return high, middle, rest - middle


def pack(value):
    return jnp.concatenate([value[:16], value[16:]], axis=1)


def kernel(
    densities, points, normals, source_basis, target_basis, upward, downward, couplings,
    coarse_couplings, near_list, far_want, far_list, far_count,
    out,
    dens, geom, wants_own, wants, asked, sbasis, tbasis, up, down, coup, coarse_coup,
    nlist, flist, fcount, skel, outgoing, received, sums,
    features, sources, rows, targets, columns, result,
    load_sem, halo_send, halo_recv, want_send, want_recv, far_send, far_recv,
    sum_send, sum_recv, out_sem,
):
    g = lax.axis_index("row")
    c = lax.axis_index("col")
    above = lax.rem(c + 1, COLS)
    below = lax.rem(c + COLS - 1, COLS)

    barrier = pltpu.get_barrier_semaphore()

    def load(source, target, place):
        copy = pltpu.make_async_copy(source, target, load_sem.at[place])
        copy.start()
        return copy

    load_points = load(points, geom.at[1, pl.ds(0, 3)], 0)
    load_normals = load(normals, geom.at[1, pl.ds(3, 3)], 1)
    load_dens = load(densities, dens.at[1], 2)
    load_wants = load(far_want, wants_own, 3)

    def greet(d, _):
        pl.semaphore_signal(
            barrier, inc=1, device_id=(g, lax.rem(c + d, COLS)), device_id_type=MESH
        )
        return 0

    def greet_row(d, _):
        pl.semaphore_signal(
            barrier, inc=1, device_id=(lax.rem(g + d, ROWS), c), device_id_type=MESH
        )
        return 0

    lax.fori_loop(1, COLS, greet, 0)
    lax.fori_loop(1, ROWS, greet_row, 0)

    load_sbasis = load(source_basis, sbasis, 4)
    load_up = load(upward, up, 5)
    load_nlist = load(near_list, nlist, 6)
    load_flist = load(far_list, flist, 7)
    load_fcount = load(far_count, fcount, 8)
    load_coup = load(couplings, coup, 9)
    load_coarse = load(coarse_couplings, coarse_coup, 10)
    load_down = load(downward, down, 11)
    load_tbasis = load(target_basis, tbasis, 12)

    load_points.wait()
    load_normals.wait()
    load_dens.wait()
    load_wants.wait()
    pl.semaphore_wait(barrier, COLS + ROWS - 2)

    halo = []
    for index, (buffer, slot, target) in enumerate(
        ((geom, 0, above), (geom, 2, below), (dens, 0, above), (dens, 2, below))
    ):
        copy = pltpu.make_async_remote_copy(
            src_ref=buffer.at[1],
            dst_ref=buffer.at[slot],
            send_sem=halo_send.at[index],
            recv_sem=halo_recv.at[index],
            device_id=(g, target),
            device_id_type=MESH,
        )
        copy.start()
        halo.append(copy)

    def send_want(d, _):
        pltpu.make_async_remote_copy(
            src_ref=wants_own,
            dst_ref=wants.at[c],
            send_sem=want_send,
            recv_sem=want_recv,
            device_id=(g, lax.rem(c + d, COLS)),
            device_id_type=MESH,
        ).start()
        return 0

    lax.fori_loop(1, COLS, send_want, 0)

    load_sbasis.wait()
    load_up.wait()
    total = jnp.zeros((RHS, RANK), f32)
    for leaf in range(LEAVES):
        value = lax.dot_general(
            dens[1, leaf], sbasis[leaf], CONTRACT_LAST, preferred_element_type=f32
        )
        rounded = value.astype(bf16)
        skel[leaf] = pack(rounded.astype(f32)).astype(bf16)
        total = total + jnp.dot(rounded, up[leaf], preferred_element_type=f32)
    sums[g] = pack(total)

    def send_sum(d, _):
        pltpu.make_async_remote_copy(
            src_ref=sums.at[g],
            dst_ref=sums.at[g],
            send_sem=sum_send,
            recv_sem=sum_recv,
            device_id=(lax.rem(g + d, ROWS), c),
            device_id_type=MESH,
        ).start()
        return 0

    lax.fori_loop(1, ROWS, send_sum, 0)

    zero = jnp.zeros((LEAVES, LEAF), f32)
    one = jnp.ones((LEAVES, LEAF), f32)

    def put(row, first, second):
        for part, value in enumerate((first, second)):
            for half in range(2):
                features[2 * part + half, pl.ds(row * LEAVES, LEAVES)] = value[
                    :, half * 128 : half * 128 + 128
                ]

    def gathered(leaf, parts):
        return jnp.concatenate(
            [features[part, pl.ds(leaf, DEPTH, stride=LEAVES), :] for part in parts], axis=1
        )

    def source_features(block):
        x, y, z = (geom[block, d].astype(f32) for d in range(3))
        nx, ny, nz = (kernel_scale * geom[block, 3 + d].astype(f32) for d in range(3))
        square = x * x + y * y + z * z + soften_square
        along = nx * x + ny * y + nz * z
        for d, value in enumerate((nx, ny, nz, along)):
            rows[d, pl.ds(block * LEAVES, LEAVES)] = value
        sh, sm, sl = split3(square)
        ah, am, al = split3(-along)
        xh, xm, xl = split3(nx)
        yh, ym, yl = split3(ny)
        zh, zm, zl = split3(nz)
        for row, (first, second) in enumerate((
            (-2.0 * x, xh), (-2.0 * y, yh), (-2.0 * z, zh), (sh, ah), (sm, am), (sl, al),
            (one, zero), (one, zero), (one, zero), (zero, xm), (zero, ym), (zero, zm),
            (zero, xl), (zero, yl), (zero, zl), (zero, zero),
        )):
            put(row, first, second)

        def one_leaf(leaf, _):
            sources[block * LEAVES + leaf] = gathered(leaf, range(4)).astype(bf16)
            return 0

        lax.fori_loop(0, LEAVES, one_leaf, 0, unroll=4)

    source_features(1)
    px, py, pz = (geom[1, d].astype(f32) for d in range(3))
    th, tm, tl = split3(px * px + py * py + pz * pz)
    for row, value in enumerate(
        (px, py, pz, one, one, one, th, tm, tl, px, py, pz, px, py, pz, zero)
    ):
        put(row, value, zero)

    def target_features(leaf, _):
        target = gathered(leaf, range(2)).T
        for d in range(3):
            columns[leaf, d] = jnp.broadcast_to(
                target[:VECTOR_ROWS, d : d + 1], (VECTOR_ROWS, 128)
            )
        targets[leaf] = target.astype(bf16)
        return 0

    lax.fori_loop(0, LEAVES, target_features, 0, unroll=2)

    def geometry(leaf, q):
        source = sources[q]
        target = targets[leaf]
        square = jnp.dot(target, source[:, :LEAF], preferred_element_type=f32)
        row = [rows[d, pl.ds(q, 1), :] for d in range(4)]
        column = [columns[leaf, d] for d in range(3)]
        parts = []
        for start in range(0, LEAF, 128):
            nx, ny, nz, along = (value[:, start : start + 128] for value in row)
            parts.append(column[0] * nx + column[1] * ny + column[2] * nz - along)
        normal = jnp.concatenate(parts, axis=1)
        rest = jnp.dot(target[VECTOR_ROWS:], source[:, LEAF:], preferred_element_type=f32)
        return square, jnp.concatenate([normal, rest], axis=0)

    def tile(square, normal):
        inverse = lax.rsqrt(square)
        return ((normal * inverse) * (inverse * inverse)).astype(bf16)

    def product(q, formed):
        return lax.dot_general(
            dens[q // LEAVES, q % LEAVES], formed, CONTRACT_LAST, preferred_element_type=f32
        )

    def near_self(group, _):
        first = group * SELF_GROUP
        held = geometry(first, LEAVES + first)
        for place in range(SELF_GROUP):
            leaf = first + place
            square, normal = held
            if place < SELF_GROUP - 1:
                held = geometry(leaf + 1, LEAVES + leaf + 1)
            result[leaf] = product(LEAVES + leaf, tile(square, normal))
        return 0

    lax.fori_loop(0, LEAVES // SELF_GROUP, near_self, 0)

    wants[c] = wants_own[...]
    requests = pltpu.make_async_remote_copy(
        src_ref=wants.at[pl.ds(0, COLS - 1)],
        dst_ref=wants.at[pl.ds(0, COLS - 1)],
        send_sem=want_send,
        recv_sem=want_recv,
        device_id=(g, above),
        device_id_type=MESH,
    )
    requests.wait_recv()
    read_wants = load(wants, asked, 13)
    halo[0].wait_recv()
    halo[1].wait_recv()
    source_features(0)
    source_features(2)
    read_wants.wait()

    def answer(d, _):
        peer = lax.rem(c + d, COLS)
        for slot in range(SLOTS):
            outgoing[SLOTS * peer + slot] = skel[asked[peer, slot, c]]
        pltpu.make_async_remote_copy(
            src_ref=outgoing.at[pl.ds(SLOTS * peer, SLOTS)],
            dst_ref=received.at[pl.ds(SLOTS * c, SLOTS)],
            send_sem=far_send,
            recv_sem=far_recv,
            device_id=(g, peer),
            device_id_type=MESH,
        ).start()
        return 0

    lax.fori_loop(1, COLS, answer, 0)
    for slot in range(SLOTS):
        received[SLOTS * c + slot] = skel[asked[c, slot, c]]

    halo[2].wait_recv()
    halo[3].wait_recv()
    load_nlist.wait()

    def near_leaves(step, _):
        first = step * NEAR_GROUP
        work = [(place, entry) for place in range(NEAR_GROUP) for entry in range(1, NEAR)]
        totals = [result[first + place] for place in range(NEAR_GROUP)]
        held = geometry(first, nlist[first, 1])
        formed = None
        for number in range(len(work) + 1):
            if number < len(work):
                square, normal = held
            if number + 1 < len(work):
                place, entry = work[number + 1]
                held = geometry(first + place, nlist[first + place, entry])
            if number:
                place, entry = work[number - 1]
                totals[place] = totals[place] + product(nlist[first + place, entry], formed)
            if number < len(work):
                formed = tile(square, normal)
        for place in range(NEAR_GROUP):
            result[first + place] = totals[place]
        return 0

    lax.fori_loop(0, LEAVES // NEAR_GROUP, near_leaves, 0)

    load_coarse.wait()
    row_sums = pltpu.make_async_remote_copy(
        src_ref=sums.at[pl.ds(0, ROWS - 1)],
        dst_ref=sums.at[pl.ds(0, ROWS - 1)],
        send_sem=sum_send,
        recv_sem=sum_recv,
        device_id=(lax.rem(g + 1, ROWS), c),
        device_id_type=MESH,
    )
    row_sums.wait_recv()
    siblings = []
    for level in range(LEVELS):
        width = 2**level
        block = g // width
        first = (block + 1 - 2 * lax.rem(block, 2)) * width
        value = sums[first]
        for other in range(1, width):
            value = value + sums[first + other]
        siblings.append(value)
    mixed = jnp.concatenate(
        [
            jnp.concatenate([value[:, :RANK] for value in siblings], axis=1),
            jnp.concatenate([value[:, RANK:] for value in siblings], axis=1),
        ],
        axis=0,
    )
    pieces = jnp.concatenate(split3(mixed), axis=0).astype(bf16)
    products = jnp.dot(
        pieces, coarse_coup[...].reshape(LEVELS * RANK, RANK), preferred_element_type=f32
    )
    field = ((products[2 * RHS :] + products[RHS : 2 * RHS]) + products[:RHS]).astype(bf16)

    load_down.wait()
    load_tbasis.wait()
    load_flist.wait()
    load_fcount.wait()
    load_coup.wait()
    arrivals = pltpu.make_async_remote_copy(
        src_ref=received.at[pl.ds(0, SLOTS * (COLS - 1))],
        dst_ref=received.at[pl.ds(0, SLOTS * (COLS - 1))],
        send_sem=far_send,
        recv_sem=far_recv,
        device_id=(g, above),
        device_id_type=MESH,
    )
    arrivals.wait_recv()

    def far_leaf(leaf, _):
        count = fcount[leaf]
        upper, lower = [], []
        for entry in range(FAR):
            value = received[flist[entry, leaf]].astype(f32)
            value = jnp.where(entry < count, value, jnp.zeros_like(value))
            upper.append(value[:, :RANK])
            lower.append(value[:, RANK:])
        chosen = jnp.concatenate(
            [jnp.concatenate(upper, axis=1), jnp.concatenate(lower, axis=1)], axis=0
        ).astype(bf16)
        coeff = jnp.dot(
            chosen, coup[leaf].reshape(FAR * RANK, RANK), preferred_element_type=f32
        ) + jnp.dot(field, down[leaf], preferred_element_type=f32)
        result[leaf] = result[leaf] + jnp.dot(
            coeff.astype(bf16), tbasis[leaf], preferred_element_type=f32
        )
        return 0

    lax.fori_loop(0, LEAVES, far_leaf, 0, unroll=4)
    store = pltpu.make_async_copy(result, out, out_sem)
    store.start()

    for copy in halo:
        copy.wait_send()
    arrivals.wait_send()

    requests.wait_send()
    row_sums.wait_send()
    store.wait()


def local(
    densities, points, normals, source_basis, target_basis, upward, downward, couplings,
    coarse_couplings, near_list, far_want, far_list, far_count,
):
    anywhere = pl.BlockSpec(memory_space=pl.ANY)
    dma = pltpu.SemaphoreType.DMA
    return pl.pallas_call(
        kernel,
        out_shape=jax.ShapeDtypeStruct((LEAVES, RHS, LEAF), f32),
        in_specs=[anywhere] * 13,
        out_specs=anywhere,
        scratch_shapes=[
            pltpu.VMEM((3, LEAVES, RHS, LEAF), bf16),
            pltpu.VMEM((3, 6, LEAVES, LEAF), bf16),
            pltpu.VMEM((SLOTS, COLS), jnp.int32),
            pltpu.VMEM((COLS, SLOTS, COLS), jnp.int32),
            pltpu.SMEM((COLS, SLOTS, COLS), jnp.int32),
            pltpu.VMEM((LEAVES, RANK, LEAF), bf16),
            pltpu.VMEM((LEAVES, RANK, LEAF), bf16),
            pltpu.VMEM((LEAVES, RANK, RANK), bf16),
            pltpu.VMEM((LEAVES, RANK, RANK), bf16),
            pltpu.VMEM((LEAVES, FAR, RANK, RANK), bf16),
            pltpu.VMEM((LEVELS, RANK, RANK), bf16),
            pltpu.SMEM((LEAVES, NEAR), jnp.int32),
            pltpu.SMEM((FAR, LEAVES), jnp.int32),
            pltpu.SMEM((LEAVES,), jnp.int32),
            pltpu.VMEM((LEAVES, 16, 128), bf16),
            pltpu.VMEM((SLOTS * COLS, 16, 128), bf16),
            pltpu.VMEM((SLOTS * COLS, 16, 128), bf16),
            pltpu.VMEM((ROWS, 16, 128), f32),
            pltpu.VMEM((4, DEPTH * LEAVES, 128), f32),
            pltpu.VMEM((3 * LEAVES, DEPTH, 2 * LEAF), bf16),
            pltpu.VMEM((4, 3 * LEAVES, LEAF), f32),
            pltpu.VMEM((LEAVES, LEAF, DEPTH), bf16),
            pltpu.VMEM((LEAVES, 3, VECTOR_ROWS, 128), f32),
            pltpu.VMEM((LEAVES, RHS, LEAF), f32),
            dma((14,)), dma((4,)), dma((4,)), dma, dma, dma, dma, dma, dma, dma,
        ],
        compiler_params=pltpu.CompilerParams(
            collective_id=0, has_side_effects=True, vmem_limit_bytes=60 * 2**20
        ),
        cost_estimate=pl.CostEstimate(
            flops=2 * 16 * 12 * 65536 * 192, bytes_accessed=6 * 2**20, transcendentals=16 * 12 * 65536
        ),
        name="h2_product",
    )(
        densities,
        points.transpose(1, 0, 2),
        normals.transpose(1, 0, 2),
        source_basis,
        target_basis,
        upward,
        downward,
        couplings,
        coarse_couplings.reshape(LEVELS, RANK, RANK),
        near_list,
        far_want.reshape(COLS, SLOTS).T,
        far_list.T,
        far_count,
    )


def solution(mesh):
    leaf = P(("row", "col"), None, None)
    placed = (
        (leaf,) * 7
        + (P(("row", "col"), None, None, None), P("row", "col", None, None, None))
        + (P(("row", "col"), None), P("row", "col", None, None))
        + (P(("row", "col"), None), P(("row", "col")))
    )
    return jax.shard_map(local, mesh=mesh, in_specs=placed, out_specs=leaf, check_vma=False)
```

```python
import math

import jax
import jax.numpy as jnp
from jax import lax
from jax.experimental import pallas as pl
from jax.experimental.pallas import tpu as pltpu
from jax.sharding import PartitionSpec as P

soften_square = 0.0025
kernel_scale = 0.25 / math.pi

LEAVES = 16
RHS = 32
RANK = 64
LEAF = 256
NEAR = 12
FAR = 8
SLOTS = 2
LEVELS = 4
ROWS = 16
COLS = 64
PEER_GROUP = 7
PEER_GROUPS = (COLS - 1) // PEER_GROUP
DEPTH = 16
SELF_GROUP = 8
NEAR_GROUP = 4
VECTOR_ROWS = 128

f32 = jnp.float32
bf16 = jnp.bfloat16
MESH = pl.DeviceIdType.MESH
CONTRACT_LAST = (((1,), (1,)), ((), ()))


def split3(value):
    high = value.astype(bf16).astype(f32)
    rest = value - high
    middle = rest.astype(bf16).astype(f32)
    return high, middle, rest - middle


def pack(value):
    return jnp.concatenate([value[:16], value[16:]], axis=1)


def kernel(
    densities, points, normals, source_basis, target_basis, upward, downward, couplings,
    coarse_couplings, near_list, far_want, far_list, far_count,
    out,
    dens, geom, wants_own, wants, asked_own, asked, sbasis, tbasis, up, down, coup, coarse_coup,
    nlist, flist, fcount, skel, outgoing, received, sums,
    features, sources, rows, targets, columns, result,
    load_sem, read_sem, halo_send, halo_recv, want_send, want_recv, far_send, far_recv,
    sum_send, sum_recv, out_sem,
):
    g = lax.axis_index("row")
    c = lax.axis_index("col")
    above = lax.rem(c + 1, COLS)
    below = lax.rem(c + COLS - 1, COLS)

    barrier = pltpu.get_barrier_semaphore()

    def load(source, target, place):
        copy = pltpu.make_async_copy(source, target, load_sem.at[place])
        copy.start()
        return copy

    load_points = load(points, geom.at[1, pl.ds(0, 3)], 0)
    load_normals = load(normals, geom.at[1, pl.ds(3, 3)], 1)
    load_dens = load(densities, dens.at[1], 2)
    load_wants = load(far_want, wants_own, 3)
    load_asked = load(far_want, asked_own, 13)

    def offset(number):
        return COLS // 2 + ((number + 1) // 2) * (1 - 2 * lax.rem(number, 2))

    def each_group(act):
        def one_group(group, _):
            for place in range(PEER_GROUP):
                act(group, group * PEER_GROUP + place)
            return 0

        lax.fori_loop(0, PEER_GROUPS, one_group, 0)

    def greet(d, _):
        pl.semaphore_signal(
            barrier, inc=1, device_id=(g, lax.rem(c + d, COLS)), device_id_type=MESH
        )
        return 0

    def greet_row(d, _):
        pl.semaphore_signal(
            barrier, inc=1, device_id=(lax.rem(g + d, ROWS), c), device_id_type=MESH
        )
        return 0

    lax.fori_loop(1, COLS, greet, 0)
    lax.fori_loop(1, ROWS, greet_row, 0)

    load_sbasis = load(source_basis, sbasis, 4)
    load_up = load(upward, up, 5)
    load_nlist = load(near_list, nlist, 6)
    load_flist = load(far_list, flist, 7)
    load_fcount = load(far_count, fcount, 8)
    load_coup = load(couplings, coup, 9)
    load_coarse = load(coarse_couplings, coarse_coup, 10)
    load_down = load(downward, down, 11)
    load_tbasis = load(target_basis, tbasis, 12)

    load_points.wait()
    load_normals.wait()
    load_dens.wait()

    load_sbasis.wait()
    load_up.wait()
    total = jnp.zeros((RHS, RANK), f32)
    for leaf in range(LEAVES):
        value = lax.dot_general(
            dens[1, leaf], sbasis[leaf], CONTRACT_LAST, preferred_element_type=f32
        )
        rounded = value.astype(bf16)
        skel[leaf] = pack(rounded.astype(f32)).astype(bf16)
        total = total + jnp.dot(rounded, up[leaf], preferred_element_type=f32)
    sums[g] = pack(total)

    load_wants.wait()
    pl.semaphore_wait(barrier, COLS + ROWS - 2)

    def send_want(group, number):
        pltpu.make_async_remote_copy(
            src_ref=wants_own,
            dst_ref=wants.at[number],
            send_sem=want_send,
            recv_sem=want_recv.at[group],
            device_id=(g, lax.rem(c + offset(number), COLS)),
            device_id_type=MESH,
        ).start()

    each_group(send_want)

    halo = []
    for index, (buffer, slot, target) in enumerate(
        ((geom, 0, above), (geom, 2, below), (dens, 0, above), (dens, 2, below))
    ):
        copy = pltpu.make_async_remote_copy(
            src_ref=buffer.at[1],
            dst_ref=buffer.at[slot],
            send_sem=halo_send.at[index],
            recv_sem=halo_recv.at[index],
            device_id=(g, target),
            device_id_type=MESH,
        )
        copy.start()
        halo.append(copy)

    def send_sum(d, _):
        pltpu.make_async_remote_copy(
            src_ref=sums.at[g],
            dst_ref=sums.at[g],
            send_sem=sum_send,
            recv_sem=sum_recv,
            device_id=(lax.rem(g + d, ROWS), c),
            device_id_type=MESH,
        ).start()
        return 0

    lax.fori_loop(1, ROWS, send_sum, 0)

    zero = jnp.zeros((LEAVES, LEAF), f32)
    one = jnp.ones((LEAVES, LEAF), f32)

    def put(row, first, second):
        for part, value in enumerate((first, second)):
            for half in range(2):
                features[2 * part + half, pl.ds(row * LEAVES, LEAVES)] = value[
                    :, half * 128 : half * 128 + 128
                ]

    def gathered(leaf, parts):
        return jnp.concatenate(
            [features[part, pl.ds(leaf, DEPTH, stride=LEAVES), :] for part in parts], axis=1
        )

    def source_features(block):
        x, y, z = (geom[block, d].astype(f32) for d in range(3))
        nx, ny, nz = (kernel_scale * geom[block, 3 + d].astype(f32) for d in range(3))
        square = x * x + y * y + z * z + soften_square
        along = nx * x + ny * y + nz * z
        for d, value in enumerate((nx, ny, nz, along)):
            rows[d, pl.ds(block * LEAVES, LEAVES)] = value
        sh, sm, sl = split3(square)
        ah, am, al = split3(-along)
        xh, xm, xl = split3(nx)
        yh, ym, yl = split3(ny)
        zh, zm, zl = split3(nz)
        for row, (first, second) in enumerate((
            (-2.0 * x, xh), (-2.0 * y, yh), (-2.0 * z, zh), (sh, ah), (sm, am), (sl, al),
            (one, zero), (one, zero), (one, zero), (zero, xm), (zero, ym), (zero, zm),
            (zero, xl), (zero, yl), (zero, zl), (zero, zero),
        )):
            put(row, first, second)

        def one_leaf(leaf, _):
            sources[block * LEAVES + leaf] = gathered(leaf, range(4)).astype(bf16)
            return 0

        lax.fori_loop(0, LEAVES, one_leaf, 0, unroll=4)

    source_features(1)
    px, py, pz = (geom[1, d].astype(f32) for d in range(3))
    th, tm, tl = split3(px * px + py * py + pz * pz)
    for row, value in enumerate(
        (px, py, pz, one, one, one, th, tm, tl, px, py, pz, px, py, pz, zero)
    ):
        put(row, value, zero)

    def target_features(leaf, _):
        target = gathered(leaf, range(2)).T
        for d in range(3):
            columns[leaf, d] = jnp.broadcast_to(
                target[:VECTOR_ROWS, d : d + 1], (VECTOR_ROWS, 128)
            )
        targets[leaf] = target.astype(bf16)
        return 0

    lax.fori_loop(0, LEAVES, target_features, 0, unroll=8)

    def geometry(leaf, q):
        source = sources[q]
        target = targets[leaf]
        square = jnp.dot(target, source[:, :LEAF], preferred_element_type=f32)
        row = [rows[d, pl.ds(q, 1), :] for d in range(4)]
        column = [columns[leaf, d] for d in range(3)]
        parts = []
        for start in range(0, LEAF, 128):
            nx, ny, nz, along = (value[:, start : start + 128] for value in row)
            parts.append(column[0] * nx + column[1] * ny + column[2] * nz - along)
        normal = jnp.concatenate(parts, axis=1)
        rest = jnp.dot(target[VECTOR_ROWS:], source[:, LEAF:], preferred_element_type=f32)
        return square, jnp.concatenate([normal, rest], axis=0)

    def tile(square, normal):
        inverse = lax.rsqrt(square)
        return ((normal * inverse) * (inverse * inverse)).astype(bf16)

    def product(q, formed):
        return lax.dot_general(
            dens[q // LEAVES, q % LEAVES], formed, CONTRACT_LAST, preferred_element_type=f32
        )

    def near_self(group, _):
        first = group * SELF_GROUP
        held = geometry(first, LEAVES + first)
        for place in range(SELF_GROUP):
            leaf = first + place
            square, normal = held
            if place < SELF_GROUP - 1:
                held = geometry(leaf + 1, LEAVES + leaf + 1)
            result[leaf] = product(LEAVES + leaf, tile(square, normal))
        return 0

    lax.fori_loop(0, LEAVES // SELF_GROUP, near_self, 0)

    load_asked.wait()

    def read_group(group):
        chosen = pl.ds(group * PEER_GROUP, PEER_GROUP)
        return pltpu.make_async_copy(wants.at[chosen], asked.at[chosen], read_sem.at[group])

    def fetch(group):
        chosen = pl.ds(group * PEER_GROUP, PEER_GROUP)
        pltpu.make_async_remote_copy(
            src_ref=wants.at[chosen],
            dst_ref=wants.at[chosen],
            send_sem=want_send,
            recv_sem=want_recv.at[group],
            device_id=(g, above),
            device_id_type=MESH,
        ).wait_recv()
        read_group(group).start()

    def answer(group):
        read_group(group).wait()
        for place in range(PEER_GROUP):
            number = group * PEER_GROUP + place
            for slot in range(SLOTS):
                outgoing[SLOTS * number + slot] = skel[asked[number, slot, c]]
            pltpu.make_async_remote_copy(
                src_ref=outgoing.at[pl.ds(SLOTS * number, SLOTS)],
                dst_ref=received.at[pl.ds(SLOTS * c, SLOTS)],
                send_sem=far_send,
                recv_sem=far_recv,
                device_id=(g, lax.rem(c + COLS - offset(number), COLS)),
                device_id_type=MESH,
            ).start()

    def fetch_one(group, _):
        fetch(group)
        return 0

    def answer_one(group, _):
        answer(group)
        return 0

    lax.fori_loop(0, PEER_GROUPS, fetch_one, 0)
    lax.fori_loop(0, PEER_GROUPS, answer_one, 0)
    for slot in range(SLOTS):
        received[SLOTS * c + slot] = skel[asked_own[slot, c]]

    halo[0].wait_recv()
    halo[1].wait_recv()
    source_features(0)
    source_features(2)
    halo[2].wait_recv()
    halo[3].wait_recv()
    load_nlist.wait()

    def near_leaves(step, _):
        first = step * NEAR_GROUP
        work = [(place, entry) for place in range(NEAR_GROUP) for entry in range(1, NEAR)]
        totals = [result[first + place] for place in range(NEAR_GROUP)]
        held = geometry(first, nlist[first, 1])
        formed = None
        for number in range(len(work) + 1):
            if number < len(work):
                square, normal = held
            if number + 1 < len(work):
                place, entry = work[number + 1]
                held = geometry(first + place, nlist[first + place, entry])
            if number:
                place, entry = work[number - 1]
                totals[place] = totals[place] + product(nlist[first + place, entry], formed)
            if number < len(work):
                formed = tile(square, normal)
        for place in range(NEAR_GROUP):
            result[first + place] = totals[place]
        return 0

    lax.fori_loop(0, LEAVES // NEAR_GROUP, near_leaves, 0)

    load_coarse.wait()
    row_sums = pltpu.make_async_remote_copy(
        src_ref=sums.at[pl.ds(0, ROWS - 1)],
        dst_ref=sums.at[pl.ds(0, ROWS - 1)],
        send_sem=sum_send,
        recv_sem=sum_recv,
        device_id=(lax.rem(g + 1, ROWS), c),
        device_id_type=MESH,
    )
    row_sums.wait_recv()
    siblings = []
    for level in range(LEVELS):
        width = 2**level
        block = g // width
        first = (block + 1 - 2 * lax.rem(block, 2)) * width
        value = sums[first]
        for other in range(1, width):
            value = value + sums[first + other]
        siblings.append(value)
    mixed = jnp.concatenate(
        [
            jnp.concatenate([value[:, :RANK] for value in siblings], axis=1),
            jnp.concatenate([value[:, RANK:] for value in siblings], axis=1),
        ],
        axis=0,
    )
    pieces = jnp.concatenate(split3(mixed), axis=0).astype(bf16)
    products = jnp.dot(
        pieces, coarse_coup[...].reshape(LEVELS * RANK, RANK), preferred_element_type=f32
    )
    field = ((products[2 * RHS :] + products[RHS : 2 * RHS]) + products[:RHS]).astype(bf16)

    load_down.wait()
    load_tbasis.wait()
    load_flist.wait()
    load_fcount.wait()
    load_coup.wait()
    arrivals = pltpu.make_async_remote_copy(
        src_ref=received.at[pl.ds(0, SLOTS * (COLS - 1))],
        dst_ref=received.at[pl.ds(0, SLOTS * (COLS - 1))],
        send_sem=far_send,
        recv_sem=far_recv,
        device_id=(g, above),
        device_id_type=MESH,
    )
    arrivals.wait_recv()

    def far_leaf(leaf, _):
        count = fcount[leaf]
        upper, lower = [], []
        for entry in range(FAR):
            value = received[flist[entry, leaf]].astype(f32)
            value = jnp.where(entry < count, value, jnp.zeros_like(value))
            upper.append(value[:, :RANK])
            lower.append(value[:, RANK:])
        chosen = jnp.concatenate(
            [jnp.concatenate(upper, axis=1), jnp.concatenate(lower, axis=1)], axis=0
        ).astype(bf16)
        coeff = jnp.dot(
            chosen, coup[leaf].reshape(FAR * RANK, RANK), preferred_element_type=f32
        ) + jnp.dot(field, down[leaf], preferred_element_type=f32)
        result[leaf] = result[leaf] + jnp.dot(
            coeff.astype(bf16), tbasis[leaf], preferred_element_type=f32
        )
        return 0

    lax.fori_loop(0, LEAVES, far_leaf, 0, unroll=8)
    store = pltpu.make_async_copy(result, out, out_sem)
    store.start()

    for copy in halo:
        copy.wait_send()
    arrivals.wait_send()

    pltpu.make_async_remote_copy(
        src_ref=wants.at[pl.ds(0, COLS - 1)],
        dst_ref=wants.at[pl.ds(0, COLS - 1)],
        send_sem=want_send,
        recv_sem=want_recv.at[0],
        device_id=(g, above),
        device_id_type=MESH,
    ).wait_send()
    row_sums.wait_send()
    store.wait()


def local(
    densities, points, normals, source_basis, target_basis, upward, downward, couplings,
    coarse_couplings, near_list, far_want, far_list, far_count,
):
    anywhere = pl.BlockSpec(memory_space=pl.ANY)
    dma = pltpu.SemaphoreType.DMA
    return pl.pallas_call(
        kernel,
        out_shape=jax.ShapeDtypeStruct((LEAVES, RHS, LEAF), f32),
        in_specs=[anywhere] * 13,
        out_specs=anywhere,
        scratch_shapes=[
            pltpu.VMEM((3, LEAVES, RHS, LEAF), bf16),
            pltpu.VMEM((3, 6, LEAVES, LEAF), bf16),
            pltpu.VMEM((SLOTS, COLS), jnp.int32),
            pltpu.VMEM((COLS - 1, SLOTS, COLS), jnp.int32),
            pltpu.SMEM((SLOTS, COLS), jnp.int32),
            pltpu.SMEM((COLS - 1, SLOTS, COLS), jnp.int32),
            pltpu.VMEM((LEAVES, RANK, LEAF), bf16),
            pltpu.VMEM((LEAVES, RANK, LEAF), bf16),
            pltpu.VMEM((LEAVES, RANK, RANK), bf16),
            pltpu.VMEM((LEAVES, RANK, RANK), bf16),
            pltpu.VMEM((LEAVES, FAR, RANK, RANK), bf16),
            pltpu.VMEM((LEVELS, RANK, RANK), bf16),
            pltpu.SMEM((LEAVES, NEAR), jnp.int32),
            pltpu.SMEM((FAR, LEAVES), jnp.int32),
            pltpu.SMEM((LEAVES,), jnp.int32),
            pltpu.VMEM((LEAVES, 16, 128), bf16),
            pltpu.VMEM((SLOTS * (COLS - 1), 16, 128), bf16),
            pltpu.VMEM((SLOTS * COLS, 16, 128), bf16),
            pltpu.VMEM((ROWS, 16, 128), f32),
            pltpu.VMEM((4, DEPTH * LEAVES, 128), f32),
            pltpu.VMEM((3 * LEAVES, DEPTH, 2 * LEAF), bf16),
            pltpu.VMEM((4, 3 * LEAVES, LEAF), f32),
            pltpu.VMEM((LEAVES, LEAF, DEPTH), bf16),
            pltpu.VMEM((LEAVES, 3, VECTOR_ROWS, 128), f32),
            pltpu.VMEM((LEAVES, RHS, LEAF), f32),
            dma((14,)), dma((PEER_GROUPS,)), dma((4,)), dma((4,)), dma, dma((PEER_GROUPS,)),
            dma, dma, dma, dma, dma,
        ],
        compiler_params=pltpu.CompilerParams(
            collective_id=0, has_side_effects=True, vmem_limit_bytes=60 * 2**20
        ),
        cost_estimate=pl.CostEstimate(
            flops=2 * 16 * 12 * 65536 * 192, bytes_accessed=6 * 2**20, transcendentals=16 * 12 * 65536
        ),
        name="h2_product",
    )(
        densities,
        points.transpose(1, 0, 2),
        normals.transpose(1, 0, 2),
        source_basis,
        target_basis,
        upward,
        downward,
        couplings,
        coarse_couplings.reshape(LEVELS, RANK, RANK),
        near_list,
        far_want.reshape(COLS, SLOTS).T,
        far_list.T,
        far_count,
    )


def solution(mesh):
    leaf = P(("row", "col"), None, None)
    placed = (
        (leaf,) * 7
        + (P(("row", "col"), None, None, None), P("row", "col", None, None, None))
        + (P(("row", "col"), None), P("row", "col", None, None))
        + (P(("row", "col"), None), P(("row", "col")))
    )
    return jax.shard_map(local, mesh=mesh, in_specs=placed, out_specs=leaf, check_vma=False)
```

```python
import math

import jax
import jax.numpy as jnp
from jax import lax
from jax.experimental import pallas as pl
from jax.experimental.pallas import tpu as pltpu
from jax.sharding import PartitionSpec as P

soften_square = 0.0025
kernel_scale = 0.25 / math.pi

LEAVES = 16
RHS = 32
RANK = 64
LEAF = 256
NEAR = 12
FAR = 8
SLOTS = 2
LEVELS = 4
ROWS = 16
COLS = 64
PEER_GROUP = 7
PEER_GROUPS = (COLS - 1) // PEER_GROUP
DEPTH = 16
SELF_GROUP = 8
NEAR_GROUP = 4
VECTOR_ROWS = 96

f32 = jnp.float32
bf16 = jnp.bfloat16
MESH = pl.DeviceIdType.MESH
CONTRACT_LAST = (((1,), (1,)), ((), ()))


def split3(value):
    high = value.astype(bf16).astype(f32)
    rest = value - high
    middle = rest.astype(bf16).astype(f32)
    return high, middle, rest - middle


def pack(value):
    return jnp.concatenate([value[:16], value[16:]], axis=1)


def kernel(
    densities, points, normals, source_basis, target_basis, upward, downward, couplings,
    coarse_couplings, near_list, far_want, far_list, far_count,
    out,
    dens, geom, wants_own, wants, asked_own, asked, sbasis, tbasis, up, down, coup, coarse_coup,
    nlist, flist, fcount, skel, outgoing, received, sums,
    features, sources, rows, targets, columns, result,
    load_sem, read_sem, halo_send, halo_recv, want_send, want_recv, far_send, far_recv,
    sum_send, sum_recv, out_sem,
):
    g = lax.axis_index("row")
    c = lax.axis_index("col")
    above = lax.rem(c + 1, COLS)
    below = lax.rem(c + COLS - 1, COLS)

    barrier = pltpu.get_barrier_semaphore()

    def load(source, target, place):
        copy = pltpu.make_async_copy(source, target, load_sem.at[place])
        copy.start()
        return copy

    load_points = load(points, geom.at[1, pl.ds(0, 3)], 0)
    load_normals = load(normals, geom.at[1, pl.ds(3, 3)], 1)
    load_dens = load(densities, dens.at[1], 2)
    load_wants = load(far_want, wants_own, 3)
    load_asked = load(far_want, asked_own, 13)

    def offset(number):
        return COLS // 2 + ((number + 1) // 2) * (1 - 2 * lax.rem(number, 2))

    def each_group(act):
        def one_group(group, _):
            for place in range(PEER_GROUP):
                act(group, group * PEER_GROUP + place)
            return 0

        lax.fori_loop(0, PEER_GROUPS, one_group, 0)

    def greet(d, _):
        pl.semaphore_signal(
            barrier, inc=1, device_id=(g, lax.rem(c + d, COLS)), device_id_type=MESH
        )
        return 0

    def greet_row(d, _):
        pl.semaphore_signal(
            barrier, inc=1, device_id=(lax.rem(g + d, ROWS), c), device_id_type=MESH
        )
        return 0

    lax.fori_loop(1, COLS, greet, 0)
    lax.fori_loop(1, ROWS, greet_row, 0)

    load_sbasis = load(source_basis, sbasis, 4)
    load_up = load(upward, up, 5)
    load_nlist = load(near_list, nlist, 6)
    load_flist = load(far_list, flist, 7)
    load_fcount = load(far_count, fcount, 8)
    load_coup = load(couplings, coup, 9)
    load_coarse = load(coarse_couplings, coarse_coup, 10)
    load_down = load(downward, down, 11)
    load_tbasis = load(target_basis, tbasis, 12)

    load_points.wait()
    load_normals.wait()
    load_dens.wait()

    load_sbasis.wait()
    load_up.wait()
    total = jnp.zeros((RHS, RANK), f32)
    for leaf in range(LEAVES):
        value = lax.dot_general(
            dens[1, leaf], sbasis[leaf], CONTRACT_LAST, preferred_element_type=f32
        )
        rounded = value.astype(bf16)
        skel[leaf] = pack(rounded.astype(f32)).astype(bf16)
        total = total + jnp.dot(rounded, up[leaf], preferred_element_type=f32)
    sums[g] = pack(total)

    load_wants.wait()
    pl.semaphore_wait(barrier, COLS + ROWS - 2)

    def send_want(group, number):
        pltpu.make_async_remote_copy(
            src_ref=wants_own,
            dst_ref=wants.at[number],
            send_sem=want_send,
            recv_sem=want_recv.at[group],
            device_id=(g, lax.rem(c + offset(number), COLS)),
            device_id_type=MESH,
        ).start()

    each_group(send_want)

    halo = []
    for index, (buffer, slot, target) in enumerate(
        ((geom, 0, above), (geom, 2, below), (dens, 0, above), (dens, 2, below))
    ):
        copy = pltpu.make_async_remote_copy(
            src_ref=buffer.at[1],
            dst_ref=buffer.at[slot],
            send_sem=halo_send.at[index],
            recv_sem=halo_recv.at[index],
            device_id=(g, target),
            device_id_type=MESH,
        )
        copy.start()
        halo.append(copy)

    def send_sum(d, _):
        pltpu.make_async_remote_copy(
            src_ref=sums.at[g],
            dst_ref=sums.at[g],
            send_sem=sum_send,
            recv_sem=sum_recv,
            device_id=(lax.rem(g + d, ROWS), c),
            device_id_type=MESH,
        ).start()
        return 0

    lax.fori_loop(1, ROWS, send_sum, 0)

    zero = jnp.zeros((LEAVES, LEAF), f32)
    one = jnp.ones((LEAVES, LEAF), f32)

    def put(row, first, second):
        for part, value in enumerate((first, second)):
            for half in range(2):
                features[2 * part + half, pl.ds(row * LEAVES, LEAVES)] = value[
                    :, half * 128 : half * 128 + 128
                ]

    def gathered(leaf, parts):
        return jnp.concatenate(
            [features[part, pl.ds(leaf, DEPTH, stride=LEAVES), :] for part in parts], axis=1
        )

    def source_features(block):
        x, y, z = (geom[block, d].astype(f32) for d in range(3))
        nx, ny, nz = (kernel_scale * geom[block, 3 + d].astype(f32) for d in range(3))
        square = x * x + y * y + z * z + soften_square
        along = nx * x + ny * y + nz * z
        for d, value in enumerate((nx, ny, nz, along)):
            rows[d, pl.ds(block * LEAVES, LEAVES)] = value
        sh, sm, sl = split3(square)
        ah, am, al = split3(-along)
        xh, xm, xl = split3(nx)
        yh, ym, yl = split3(ny)
        zh, zm, zl = split3(nz)
        for row, (first, second) in enumerate((
            (-2.0 * x, xh), (-2.0 * y, yh), (-2.0 * z, zh), (sh, ah), (sm, am), (sl, al),
            (one, zero), (one, zero), (one, zero), (zero, xm), (zero, ym), (zero, zm),
            (zero, xl), (zero, yl), (zero, zl), (zero, zero),
        )):
            put(row, first, second)

        def one_leaf(leaf, _):
            sources[block * LEAVES + leaf] = gathered(leaf, range(4)).astype(bf16)
            return 0

        lax.fori_loop(0, LEAVES, one_leaf, 0, unroll=4)

    source_features(1)
    px, py, pz = (geom[1, d].astype(f32) for d in range(3))
    th, tm, tl = split3(px * px + py * py + pz * pz)
    for row, value in enumerate(
        (px, py, pz, one, one, one, th, tm, tl, px, py, pz, px, py, pz, zero)
    ):
        put(row, value, zero)

    def target_features(leaf, _):
        target = gathered(leaf, range(2)).T
        for d in range(3):
            columns[leaf, d] = jnp.broadcast_to(
                target[:VECTOR_ROWS, d : d + 1], (VECTOR_ROWS, 128)
            )
        targets[leaf] = target.astype(bf16)
        return 0

    lax.fori_loop(0, LEAVES, target_features, 0, unroll=8)

    def geometry(leaf, q):
        source = sources[q]
        target = targets[leaf]
        square = jnp.dot(target, source[:, :LEAF], preferred_element_type=f32)
        row = [rows[d, pl.ds(q, 1), :] for d in range(4)]
        column = [columns[leaf, d] for d in range(3)]
        parts = []
        for start in range(0, LEAF, 128):
            nx, ny, nz, along = (value[:, start : start + 128] for value in row)
            parts.append(column[0] * nx + column[1] * ny + column[2] * nz - along)
        normal = jnp.concatenate(parts, axis=1)
        rest = jnp.dot(target[VECTOR_ROWS:], source[:, LEAF:], preferred_element_type=f32)
        return square, jnp.concatenate([normal, rest], axis=0)

    def tile(square, normal):
        inverse = lax.rsqrt(square)
        return ((normal * inverse) * (inverse * inverse)).astype(bf16)

    def product(q, formed):
        return lax.dot_general(
            dens[q // LEAVES, q % LEAVES], formed, CONTRACT_LAST, preferred_element_type=f32
        )

    def near_self(group, _):
        first = group * SELF_GROUP
        held = geometry(first, LEAVES + first)
        for place in range(SELF_GROUP):
            leaf = first + place
            square, normal = held
            if place < SELF_GROUP - 1:
                held = geometry(leaf + 1, LEAVES + leaf + 1)
            result[leaf] = product(LEAVES + leaf, tile(square, normal))
        return 0

    lax.fori_loop(0, LEAVES // SELF_GROUP, near_self, 0)

    load_asked.wait()

    def read_group(group):
        chosen = pl.ds(group * PEER_GROUP, PEER_GROUP)
        return pltpu.make_async_copy(wants.at[chosen], asked.at[chosen], read_sem.at[group])

    def fetch(group):
        chosen = pl.ds(group * PEER_GROUP, PEER_GROUP)
        pltpu.make_async_remote_copy(
            src_ref=wants.at[chosen],
            dst_ref=wants.at[chosen],
            send_sem=want_send,
            recv_sem=want_recv.at[group],
            device_id=(g, above),
            device_id_type=MESH,
        ).wait_recv()
        read_group(group).start()

    def answer(group):
        read_group(group).wait()
        for place in range(PEER_GROUP):
            number = group * PEER_GROUP + place
            for slot in range(SLOTS):
                outgoing[SLOTS * number + slot] = skel[asked[number, slot, c]]
            pltpu.make_async_remote_copy(
                src_ref=outgoing.at[pl.ds(SLOTS * number, SLOTS)],
                dst_ref=received.at[pl.ds(SLOTS * c, SLOTS)],
                send_sem=far_send,
                recv_sem=far_recv,
                device_id=(g, lax.rem(c + COLS - offset(number), COLS)),
                device_id_type=MESH,
            ).start()

    def fetch_one(group, _):
        fetch(group)
        return 0

    def answer_one(group, _):
        answer(group)
        return 0

    lax.fori_loop(0, PEER_GROUPS, fetch_one, 0)
    lax.fori_loop(0, PEER_GROUPS, answer_one, 0)
    for slot in range(SLOTS):
        received[SLOTS * c + slot] = skel[asked_own[slot, c]]

    halo[0].wait_recv()
    halo[1].wait_recv()
    source_features(0)
    source_features(2)
    halo[2].wait_recv()
    halo[3].wait_recv()
    load_nlist.wait()

    def near_leaves(step, _):
        first = step * NEAR_GROUP
        work = [(place, entry) for place in range(NEAR_GROUP) for entry in range(1, NEAR)]
        totals = [result[first + place] for place in range(NEAR_GROUP)]
        held = geometry(first, nlist[first, 1])
        formed = None
        for number in range(len(work) + 1):
            if number < len(work):
                square, normal = held
            if number + 1 < len(work):
                place, entry = work[number + 1]
                held = geometry(first + place, nlist[first + place, entry])
            if number:
                place, entry = work[number - 1]
                totals[place] = totals[place] + product(nlist[first + place, entry], formed)
            if number < len(work):
                formed = tile(square, normal)
        for place in range(NEAR_GROUP):
            result[first + place] = totals[place]
        return 0

    lax.fori_loop(0, LEAVES // NEAR_GROUP, near_leaves, 0)

    load_coarse.wait()
    row_sums = pltpu.make_async_remote_copy(
        src_ref=sums.at[pl.ds(0, ROWS - 1)],
        dst_ref=sums.at[pl.ds(0, ROWS - 1)],
        send_sem=sum_send,
        recv_sem=sum_recv,
        device_id=(lax.rem(g + 1, ROWS), c),
        device_id_type=MESH,
    )
    row_sums.wait_recv()
    siblings = []
    for level in range(LEVELS):
        width = 2**level
        block = g // width
        first = (block + 1 - 2 * lax.rem(block, 2)) * width
        value = sums[first]
        for other in range(1, width):
            value = value + sums[first + other]
        siblings.append(value)
    mixed = jnp.concatenate(
        [
            jnp.concatenate([value[:, :RANK] for value in siblings], axis=1),
            jnp.concatenate([value[:, RANK:] for value in siblings], axis=1),
        ],
        axis=0,
    )
    pieces = jnp.concatenate(split3(mixed), axis=0).astype(bf16)
    products = jnp.dot(
        pieces, coarse_coup[...].reshape(LEVELS * RANK, RANK), preferred_element_type=f32
    )
    field = ((products[2 * RHS :] + products[RHS : 2 * RHS]) + products[:RHS]).astype(bf16)

    load_down.wait()
    load_tbasis.wait()
    load_flist.wait()
    load_fcount.wait()
    load_coup.wait()
    arrivals = pltpu.make_async_remote_copy(
        src_ref=received.at[pl.ds(0, SLOTS * (COLS - 1))],
        dst_ref=received.at[pl.ds(0, SLOTS * (COLS - 1))],
        send_sem=far_send,
        recv_sem=far_recv,
        device_id=(g, above),
        device_id_type=MESH,
    )
    arrivals.wait_recv()

    def far_leaf(leaf, _):
        count = fcount[leaf]
        upper, lower = [], []
        for entry in range(FAR):
            value = received[flist[entry, leaf]].astype(f32)
            value = jnp.where(entry < count, value, jnp.zeros_like(value))
            upper.append(value[:, :RANK])
            lower.append(value[:, RANK:])
        chosen = jnp.concatenate(
            [jnp.concatenate(upper, axis=1), jnp.concatenate(lower, axis=1)], axis=0
        ).astype(bf16)
        coeff = jnp.dot(
            chosen, coup[leaf].reshape(FAR * RANK, RANK), preferred_element_type=f32
        ) + jnp.dot(field, down[leaf], preferred_element_type=f32)
        result[leaf] = result[leaf] + jnp.dot(
            coeff.astype(bf16), tbasis[leaf], preferred_element_type=f32
        )
        return 0

    lax.fori_loop(0, LEAVES, far_leaf, 0, unroll=8)
    store = pltpu.make_async_copy(result, out, out_sem)
    store.start()

    for copy in halo:
        copy.wait_send()
    arrivals.wait_send()

    pltpu.make_async_remote_copy(
        src_ref=wants.at[pl.ds(0, COLS - 1)],
        dst_ref=wants.at[pl.ds(0, COLS - 1)],
        send_sem=want_send,
        recv_sem=want_recv.at[0],
        device_id=(g, above),
        device_id_type=MESH,
    ).wait_send()
    row_sums.wait_send()
    store.wait()


def local(
    densities, points, normals, source_basis, target_basis, upward, downward, couplings,
    coarse_couplings, near_list, far_want, far_list, far_count,
):
    anywhere = pl.BlockSpec(memory_space=pl.ANY)
    dma = pltpu.SemaphoreType.DMA
    return pl.pallas_call(
        kernel,
        out_shape=jax.ShapeDtypeStruct((LEAVES, RHS, LEAF), f32),
        in_specs=[anywhere] * 13,
        out_specs=anywhere,
        scratch_shapes=[
            pltpu.VMEM((3, LEAVES, RHS, LEAF), bf16),
            pltpu.VMEM((3, 6, LEAVES, LEAF), bf16),
            pltpu.VMEM((SLOTS, COLS), jnp.int32),
            pltpu.VMEM((COLS - 1, SLOTS, COLS), jnp.int32),
            pltpu.SMEM((SLOTS, COLS), jnp.int32),
            pltpu.SMEM((COLS - 1, SLOTS, COLS), jnp.int32),
            pltpu.VMEM((LEAVES, RANK, LEAF), bf16),
            pltpu.VMEM((LEAVES, RANK, LEAF), bf16),
            pltpu.VMEM((LEAVES, RANK, RANK), bf16),
            pltpu.VMEM((LEAVES, RANK, RANK), bf16),
            pltpu.VMEM((LEAVES, FAR, RANK, RANK), bf16),
            pltpu.VMEM((LEVELS, RANK, RANK), bf16),
            pltpu.SMEM((LEAVES, NEAR), jnp.int32),
            pltpu.SMEM((FAR, LEAVES), jnp.int32),
            pltpu.SMEM((LEAVES,), jnp.int32),
            pltpu.VMEM((LEAVES, 16, 128), bf16),
            pltpu.VMEM((SLOTS * (COLS - 1), 16, 128), bf16),
            pltpu.VMEM((SLOTS * COLS, 16, 128), bf16),
            pltpu.VMEM((ROWS, 16, 128), f32),
            pltpu.VMEM((4, DEPTH * LEAVES, 128), f32),
            pltpu.VMEM((3 * LEAVES, DEPTH, 2 * LEAF), bf16),
            pltpu.VMEM((4, 3 * LEAVES, LEAF), f32),
            pltpu.VMEM((LEAVES, LEAF, DEPTH), bf16),
            pltpu.VMEM((LEAVES, 3, VECTOR_ROWS, 128), f32),
            pltpu.VMEM((LEAVES, RHS, LEAF), f32),
            dma((14,)), dma((PEER_GROUPS,)), dma((4,)), dma((4,)), dma, dma((PEER_GROUPS,)),
            dma, dma, dma, dma, dma,
        ],
        compiler_params=pltpu.CompilerParams(
            collective_id=0, has_side_effects=True, vmem_limit_bytes=60 * 2**20
        ),
        cost_estimate=pl.CostEstimate(
            flops=2 * 16 * 12 * 65536 * 192, bytes_accessed=6 * 2**20, transcendentals=16 * 12 * 65536
        ),
        name="h2_product",
    )(
        densities,
        points.transpose(1, 0, 2),
        normals.transpose(1, 0, 2),
        source_basis,
        target_basis,
        upward,
        downward,
        couplings,
        coarse_couplings.reshape(LEVELS, RANK, RANK),
        near_list,
        far_want.reshape(COLS, SLOTS).T,
        far_list.T,
        far_count,
    )


def solution(mesh):
    leaf = P(("row", "col"), None, None)
    placed = (
        (leaf,) * 7
        + (P(("row", "col"), None, None, None), P("row", "col", None, None, None))
        + (P(("row", "col"), None), P("row", "col", None, None))
        + (P(("row", "col"), None), P(("row", "col")))
    )
    return jax.shard_map(local, mesh=mesh, in_specs=placed, out_specs=leaf, check_vma=False)
```
